512 devices in a mesh: expert: 8 (over z_hi, y), blk: 64 (over x, z_lo, core).
Axes of the slice: x: 4, y: 4, z: 16 (z_hi: 2, z_lo: 8; z = z_hi * 8 + z_lo), core: 2. Of those that a mesh axis runs over, the one named last changes fastest.
Arguments:
- tokens: bfloat16 [2048, 6144], P('expert', 'blk'), may hold values from -6 to 6
- expert_ids: int32 [2048, 2], P('expert'), may hold values from 0 to 7, all different within a row
- routing_weights: float32 [2048, 2], P('expert'), may hold values from 0.2 to 1
- gate_weight: bfloat16 [8, 6144, 8192], P('expert', None, 'blk'), may hold values from -0.078125 to 0.078125
- up_weight: bfloat16 [8, 6144, 8192], P('expert', None, 'blk'), may hold values from -0.078125 to 0.078125
- down_weight: bfloat16 [8, 8192, 6144], P('expert', None, 'blk'), may hold values from -0.0625 to 0.0625
Outputs:
- mixed: bfloat16 [2048, 6144], P('expert', 'blk')
The draws below stay inside these ranges and needn't reach their ends.
Inputs may be any that keep to these rules, and one draw needn't show every extreme that they name: `expert_ids`: each row names two different experts.
All inputs are finite; a program needn't handle non-finite values.
Results may differ from the reference program's by a relative error of at most 0.0057.
Values may be sent and summed in bfloat16 or wider, within the bound.
No kernel may reach another device: no remote copies, remote signals or barrier semaphores. Data moves between devices by JAX's collectives and lax.ppermute only.
A program may use at most 64 MiB of HBM per device.

```python
import jax
import jax.numpy as jnp
from jax import lax

D = 6144
FF = 8192
TOK_SHARD = 256
EXPERTS = 8
TOKENS = 2048
CAP = 64


def levels(own_key, shape, pieces, low, top_value):
    gain, own = 1.0, jax.random.fold_in(own_key, 6)
    for dim, shards_of in pieces:
        steps = jnp.exp(jax.random.uniform(jax.random.fold_in(own, dim), (shards_of,), jnp.float32, low / len(pieces), top_value / len(pieces)))
        gain = gain * jnp.repeat(steps, shape[dim] // shards_of).reshape([-1 if axis == dim else 1 for axis in range(len(shape))])
    return gain


def picks_of(own_key, rows, count, top, lift):
    ranking = jax.random.permutation(jax.random.fold_in(own_key, 1), count)
    boost = ranking
    for power in range(3):
        boost = boost * boost // count
    boost = boost * lift // count
    lots = jax.random.randint(jax.random.fold_in(own_key, 2), (rows, count), 0, 4096) + boost
    holders = jax.random.permutation(jax.random.fold_in(own_key, 3), rows)[jnp.arange(count) % rows]
    lots = jnp.where(jnp.arange(rows)[:, None] == holders[None, :], 1 << 14, lots)
    priority = lots * count + jnp.arange(count)
    return lax.top_k(priority.astype(jnp.int32), top)[1].astype(jnp.int32)


def noise(key, shape, spread, reach, cuts=(), kind=jnp.bfloat16):
    entries = spread * jax.random.normal(key, shape, jnp.float32)
    if cuts:
        entries = entries * levels(key, shape, cuts, -0.22, 0.18)
    return jnp.clip(entries, -reach, reach).astype(kind)


def setup_inputs(seed: int = 0) -> dict:
    key_of = jax.random.split(jax.random.key(seed), 7)
    tokens = noise(key_of[0], (TOKENS, D), 1.0, 6.0, ((0, 8), (1, 64)))
    expert_ids = picks_of(key_of[1], TOKENS, EXPERTS, 2, 4096)
    routing_weights = jnp.clip(0.2 + 0.8 * jax.random.uniform(key_of[2], (TOKENS, 2), jnp.float32) ** levels(key_of[2], (TOKENS, 2), ((0, 8),), -0.2, 0.2), 0.2, 1.0)
    gate_weight = noise(key_of[3], (EXPERTS, D, FF), D ** -0.5, 0.078125, ((0, 8), (2, 64)))
    up_weight = noise(key_of[4], (EXPERTS, D, FF), D ** -0.5, 0.078125, ((0, 8), (2, 64)))
    down_weight = noise(key_of[5], (EXPERTS, FF, D), FF ** -0.5, 0.0625, ((0, 8), (2, 64)))
    return {"tokens": tokens, "expert_ids": expert_ids, "routing_weights": routing_weights, "gate_weight": gate_weight, "up_weight": up_weight, "down_weight": down_weight}


def route_shard(ids, experts, capacity):
    flat = ids.reshape(-1)
    onehot = (flat[:, None] == jnp.arange(experts, dtype=jnp.int32)[None, :]).astype(jnp.int32)
    earlier = jnp.cumsum(onehot, axis=0) - onehot
    slot = jnp.sum(earlier * onehot, axis=1).reshape(ids.shape)
    return slot


def reference(tokens, expert_ids, routing_weights, gate_weight, up_weight, down_weight):
    shards = TOKENS // TOK_SHARD
    ids = expert_ids.reshape(shards, TOK_SHARD, 2)
    slot = jax.vmap(lambda block: route_shard(block, EXPERTS, CAP))(ids)
    kept = slot < CAP
    source = jnp.arange(shards, dtype=jnp.int32)[:, None, None]
    place = ids * (shards * CAP) + source * CAP + slot
    place = jnp.where(kept, place, EXPERTS * shards * CAP).astype(jnp.int32)
    rows = jnp.broadcast_to(tokens.reshape(shards, TOK_SHARD, 1, D), (shards, TOK_SHARD, 2, D))
    buffer = jnp.zeros((EXPERTS * shards * CAP, D), jnp.bfloat16)
    buffer = buffer.at[place.reshape(-1)].set(rows.reshape(-1, D), mode="drop")
    buffer = buffer.reshape(EXPERTS, shards * CAP, D)

    def one_expert(items):
        block, w_gate, w_up, w_down = items
        gate = jnp.dot(block, w_gate, preferred_element_type=jnp.float32)
        up = jnp.dot(block, w_up, preferred_element_type=jnp.float32)
        hidden = (jax.nn.silu(gate) * up).astype(jnp.bfloat16)
        return jnp.dot(hidden, w_down, preferred_element_type=jnp.float32).astype(jnp.bfloat16)

    expert_out = lax.map(one_expert, (buffer, gate_weight, up_weight, down_weight))
    flat_out = expert_out.reshape(EXPERTS * shards * CAP, D)
    safe = jnp.minimum(place, EXPERTS * shards * CAP - 1).reshape(-1)
    picked = flat_out[safe].astype(jnp.float32).reshape(shards, TOK_SHARD, 2, D)
    scale = jnp.where(kept, routing_weights.reshape(shards, TOK_SHARD, 2), jnp.float32(0.0))
    mixed = jnp.sum(picked * scale[..., None], axis=2)
    return mixed.reshape(TOKENS, D).astype(jnp.bfloat16)
```

```python
import jax
import jax.numpy as jnp
from jax import lax
from jax.sharding import Mesh, PartitionSpec as P

BF = jnp.bfloat16
F32 = jnp.float32
CAP = 64
AXES = ("zh", "y", "x", "z", "c")


def shift(n, d):
    return [(i, (i + d) % n) for i in range(n)]


def flip(n, d):
    return [(i, i ^ d) for i in range(n)]


def contract(a, b, da, db):
    return lax.dot_general(a, b, (((da,), (db,)), ((), ())), preferred_element_type=F32)


def in_order(high, own, other, axis):
    return jnp.where(
        high, jnp.stack([other, own], axis), jnp.stack([own, other], axis)
    )


def gather_z(v):
    z = lax.axis_index("z")
    for axis, step in enumerate((4, 2, 1)):
        other = lax.ppermute(v, "z", flip(8, step))
        v = in_order((z & step) != 0, v, other, axis)
    return v.reshape(-1, v.shape[-1])


def with_other_core(v, rows):
    other = lax.ppermute(v, "c", flip(2, 1))
    lanes = v.shape[-1]
    both = in_order(
        lax.axis_index("c") != 0, v.reshape(-1, rows, lanes), other.reshape(-1, rows, lanes), 1
    )
    return both.reshape(-1, lanes)


def route(expert_ids):
    ids = expert_ids.T
    expert = lax.broadcasted_iota(jnp.int32, (8, ids.shape[1]), 0)
    first = ids[0][None, :] == expert
    second = ids[1][None, :] == expert
    ones = first.astype(BF) + second.astype(BF)
    n = ids.shape[1]
    before = lax.broadcasted_iota(jnp.int32, (n, n), 0) < lax.broadcasted_iota(jnp.int32, (n, n), 1)
    earlier = contract(ones, before.astype(BF), 1, 0)
    targets = []
    for k, (mine, count) in enumerate(((first, earlier), (second, earlier + first.astype(F32)))):
        slot = jnp.sum(jnp.where(mine, count, 0.0), axis=0).astype(jnp.int32)
        targets.append(jnp.where(slot < CAP, ids[k] * CAP + slot, -1))
    return targets


def local(tokens, expert_ids, routing_weights, gate_weight, up_weight, down_weight):
    zh, x = lax.axis_index("zh"), lax.axis_index("x")
    feats = tokens.shape[1]
    down = down_weight[0].T.reshape(feats, 4, -1)
    downs = []
    for d in range(4):
        part = lax.dynamic_index_in_dim(down, (x + d) % 4, 1, keepdims=False)
        downs.append(lax.ppermute(part, "x", shift(4, d)) if d else part)

    targets = route(expert_ids)
    slot = lax.broadcasted_iota(jnp.int32, (4 * CAP, tokens.shape[0]), 0)
    hits = []
    for half in range(2):
        base = jnp.where(half == 0, zh, 1 - zh) * (4 * CAP)
        hits.append([(t[None, :] - base) == slot for t in targets])
    packed = [contract(tokens, (a | b).astype(BF), 0, 1).astype(BF) for a, b in hits]
    packed[1] = lax.ppermute(packed[1], "zh", flip(2, 1))

    gate_up = jnp.concatenate([gate_weight[0], up_weight[0]], axis=1).reshape(4, -1, 256)
    gate_ups = [lax.dynamic_index_in_dim(gate_up, (x - d) % 4, 0, keepdims=False) for d in range(4)]

    backs = [None, None]
    for half in (0, 1):
        v = lax.all_to_all(packed[half].reshape(feats, 4, CAP), "y", 1, 0)
        v = v.transpose(1, 0, 2).reshape(feats, 4 * CAP)
        v = gather_z(v)
        both = 0.0
        for d in (0, 1, 3, 2):
            piece = lax.ppermute(v, "x", shift(4, d)) if d else v
            piece = with_other_core(piece, feats)
            both = both + contract(gate_ups[d], piece, 0, 0)
        gate, up = both[:128], both[128:]
        hidden = (jax.nn.silu(gate) * up).astype(BF)
        hidden = with_other_core(gather_z(hidden), 128)
        total = 0.0
        for d in (2, 1, 3, 0):
            part = contract(downs[d], hidden, 1, 0)
            if d:
                part = lax.ppermute(part.astype(BF), "x", shift(4, -d)).astype(F32)
            total = total + part
        out = total.astype(BF)
        back = lax.all_to_all(out.reshape(feats, 4, CAP), "y", 1, 0)
        back = back.transpose(1, 0, 2).reshape(feats, 4 * CAP)
        backs[half] = lax.ppermute(back, "zh", flip(2, 1)) if half else back

    mixed = 0.0
    for k in range(2):
        picked = sum(contract(backs[h], hits[h][k].astype(BF), 1, 0) for h in range(2))
        mixed = mixed + picked * routing_weights[:, k][None, :]
    return mixed.astype(BF).T


def solution(mesh):
    fine = Mesh(mesh.devices.reshape(2, 4, 4, 8, 2), AXES)
    rows, cols = ("zh", "y"), ("x", "z", "c")
    placed = (
        P(rows, cols),
        P(rows, None),
        P(rows, None),
        P(rows, None, cols),
        P(rows, None, cols),
        P(rows, None, cols),
    )
    return jax.shard_map(local, mesh=fine, in_specs=placed, out_specs=P(rows, cols), check_vma=False)
```

```python
import jax
import jax.numpy as jnp
from jax import lax
from jax.experimental import pallas as pl
from jax.experimental.pallas import tpu as pltpu
from jax.sharding import Mesh, PartitionSpec as P

BF = jnp.bfloat16
F32 = jnp.float32
CAP = 64
AXES = ("zh", "y", "x", "z", "c")
ORDER = (0, 4, 2, 1, 5, 3, 6, 7)
PARTS = (3, 5)


def shift(n, d):
    return [(i, (i + d) % n) for i in range(n)]


def flip(n, d):
    return [(i, i ^ d) for i in range(n)]


def contract(a, b, da, db):
    return lax.dot_general(a, b, (((da,), (db,)), ((), ())), preferred_element_type=F32)


def held(*arrays):
    return lax.optimization_barrier(arrays)


def gather_z(v):
    over = lambda a, step: lax.ppermute(a, "z", flip(8, step))
    core = lambda a: lax.ppermute(a, "c", flip(2, 1))
    rows = v.shape[0]
    b4, b2 = over(v, 4), over(v, 2)
    early = jnp.concatenate([v, b4, b2])
    b6, b153 = over(b4, 2), over(early, 1)
    early_other = core(early)
    late = jnp.concatenate([b153, b6, over(b6, 1)])
    return early, early_other, late, core(late)


def block_order():
    z, c = lax.axis_index("z"), lax.axis_index("c")
    first = [(i, j) for j in (0, 1) for i in ORDER[: PARTS[0]]]
    last = [(i, j) for j in (0, 1) for i in ORDER[PARTS[0] :]]
    return jnp.stack([(z ^ i) * 2 + (c ^ j) for i, j in first + last]).astype(jnp.int32)


def ordered(order, operands, body, blocks, out_block, out_shape):
    return pl.pallas_call(
        body,
        grid_spec=pltpu.PrefetchScalarGridSpec(
            num_scalar_prefetch=1,
            grid=(4,),
            in_specs=[pl.BlockSpec(*b) for b in blocks],
            out_specs=pl.BlockSpec(out_block, lambda p, order_ref: (p,) + (0,) * (len(out_block) - 1)),
        ),
        out_shape=out_shape,
        compiler_params=pltpu.CompilerParams(vmem_limit_bytes=16 * 2**20),
        cost_estimate=pl.CostEstimate(
            flops=0, bytes_accessed=4 * sum(a.size for a in operands), transcendentals=0
        ),
    )(order, *operands)


def ordered_gate_up(order, gate, up):
    rows = gate.shape[0] // 64

    def body(order_ref, gate_ref, up_ref, out_ref):
        for r in range(16):
            out_ref[0, r, :, :128] = gate_ref[0, order_ref[r]]
            out_ref[0, r, :, 128:] = up_ref[0, order_ref[r]]

    taken = ((1, 16, rows, 128), lambda p, order_ref: (p, 0, 0, 0))
    shape = jax.ShapeDtypeStruct((4, 16, rows, 256), gate.dtype)
    operands = [w.reshape(4, 16, rows, 128) for w in (gate, up)]
    out = ordered(order, operands, body, [taken, taken], (1, 16, rows, 256), shape)
    return out.reshape(4, 16 * rows, 256)


def ordered_down(order, down):
    feats, hidden = down.shape[0], down.shape[1] // 4

    def body(order_ref, down_ref, out_ref):
        for r in range(16):
            block = pl.ds(pl.multiple_of(order_ref[r] * 128, 128), 128)
            out_ref[0, :, r * 128 : (r + 1) * 128] = down_ref[:, block]

    taken = ((feats, hidden), lambda p, order_ref: (0, p))
    shape = jax.ShapeDtypeStruct((4, feats, hidden), down.dtype)
    return ordered(order, [down], body, [taken], (1, feats, hidden), shape)


def times_parts(w, axis, parts):
    total, at = 0.0, 0
    for part in parts:
        rows = lax.slice_in_dim(w, at, at + part.shape[0], axis=axis)
        total = total + contract(rows, part, axis, 0)
        at += part.shape[0]
    return total


def route(expert_ids):
    ids = expert_ids.T
    expert = lax.broadcasted_iota(jnp.int32, (8, ids.shape[1]), 0)
    first = ids[0][None, :] == expert
    second = ids[1][None, :] == expert
    ones = first.astype(BF) + second.astype(BF)
    n = ids.shape[1]
    before = lax.broadcasted_iota(jnp.int32, (n, n), 0) < lax.broadcasted_iota(jnp.int32, (n, n), 1)
    earlier = contract(ones, before.astype(BF), 1, 0)
    targets = []
    for k, (mine, count) in enumerate(((first, earlier), (second, earlier + first.astype(F32)))):
        slot = jnp.sum(jnp.where(mine, count, 0.0), axis=0).astype(jnp.int32)
        targets.append(jnp.where(slot < CAP, ids[k] * CAP + slot, -1))
    return targets


def local(tokens, expert_ids, routing_weights, gate_weight, up_weight, down_weight):
    zh = lax.axis_index("zh")
    feats, lanes = tokens.shape[1], 2 * CAP
    order = block_order()

    targets = route(expert_ids)
    slot = lax.broadcasted_iota(jnp.int32, (4 * CAP, tokens.shape[0]), 0)
    hits = []
    for half in range(2):
        base = jnp.where(half == 0, zh, 1 - zh) * (4 * CAP)
        hits.append([(t[None, :] - base) == slot for t in targets])
    packed = [contract(tokens, (a | b).astype(BF), 0, 1).astype(BF) for a, b in hits]
    _, gate_weight, up_weight = held(packed[1][:8], gate_weight, up_weight)
    packed[1] = lax.ppermute(packed[1], "zh", flip(2, 1))
    gate_up = ordered_gate_up(order, gate_weight[0], up_weight[0])

    v = jnp.concatenate([p.reshape(feats, 4, CAP) for p in packed], axis=2).transpose(1, 0, 2)
    v = lax.all_to_all(v, "y", 0, 0).transpose(1, 0, 2).reshape(feats, -1)
    _, gate_up, down_weight = held(v[:8, :128], gate_up, down_weight)
    gate_up = lax.all_to_all(gate_up, "x", 0, 0)
    down = ordered_down(order, down_weight[0].T)
    parts = gather_z(v)
    terms = times_parts(gate_up, 1, parts).astype(BF)
    both = jnp.sum(lax.all_to_all(terms, "x", 0, 0).astype(F32), axis=0)
    gate, up = both[:128], both[128:]
    hidden = (jax.nn.silu(gate) * up).astype(BF)

    hidden, down = held(hidden, down)
    down = lax.all_to_all(down, "x", 0, 0)
    parts = gather_z(hidden)
    terms = times_parts(down, 2, parts).astype(BF)
    terms = terms.reshape(4, feats, 4, lanes).transpose(2, 0, 1, 3).reshape(16, feats, lanes)
    terms = lax.all_to_all(terms, ("y", "x"), 0, 0).reshape(4, 4, feats, lanes)
    back = jnp.sum(terms.astype(F32), axis=1).astype(BF).transpose(1, 0, 2)
    backs = [back[:, :, :CAP].reshape(feats, -1), back[:, :, CAP:].reshape(feats, -1)]
    backs[1] = lax.ppermute(backs[1], "zh", flip(2, 1))

    mixed = 0.0
    for k in range(2):
        picked = sum(contract(backs[h], hits[h][k].astype(BF), 1, 0) for h in range(2))
        mixed = mixed + picked * routing_weights[:, k][None, :]
    return mixed.astype(BF).T


def solution(mesh):
    fine = Mesh(mesh.devices.reshape(2, 4, 4, 8, 2), AXES)
    rows, cols = ("zh", "y"), ("x", "z", "c")
    placed = (
        P(rows, cols),
        P(rows, None),
        P(rows, None),
        P(rows, None, cols),
        P(rows, None, cols),
        P(rows, None, cols),
    )
    return jax.shard_map(local, mesh=fine, in_specs=placed, out_specs=P(rows, cols), check_vma=False)
```

```python
import jax
import jax.numpy as jnp
from jax import lax
from jax.experimental import pallas as pl
from jax.experimental.pallas import tpu as pltpu
from jax.sharding import Mesh, PartitionSpec as P

BF = jnp.bfloat16
F32 = jnp.float32
CAP = 64
AXES = ("zh", "y", "x", "z", "c")
ORDER = (0, 4, 2, 1, 5, 3, 6, 7)


def shift(n, d):
    return [(i, (i + d) % n) for i in range(n)]


def flip(n, d):
    return [(i, i ^ d) for i in range(n)]


def contract(a, b, da, db):
    return lax.dot_general(a, b, (((da,), (db,)), ((), ())), preferred_element_type=F32)


def held(*arrays):
    return lax.optimization_barrier(arrays)


def gather_z(v, first):
    over = lambda a, step: lax.ppermute(a, "z", flip(8, step))
    core = lambda a: lax.ppermute(a, "c", flip(2, 1))
    b4, b2, b1 = over(v, 4), over(v, 2), over(v, 1)
    early = jnp.concatenate([v, b4, b2])
    b6, b53 = over(b4, 2), over(early[v.shape[0] :], 1)
    b153 = jnp.concatenate([b1, b53])
    late = [b153, b6, over(b6, 1)]
    if first == len(ORDER):
        rows = [jnp.concatenate([early] + late)]
        return rows[0], core(rows[0])
    late, early_other = held(jnp.concatenate(late), core(early))
    return early, early_other, late, core(late)


def block_order(first):
    z, c = lax.axis_index("z"), lax.axis_index("c")
    blocks = [(i, j) for some in (ORDER[:first], ORDER[first:]) for j in (0, 1) for i in some]
    return jnp.stack([(z ^ i) * 2 + (c ^ j) for i, j in blocks]).astype(jnp.int32)


def ordered(order, operands, body, blocks, out_block, out_shape):
    return pl.pallas_call(
        body,
        grid_spec=pltpu.PrefetchScalarGridSpec(
            num_scalar_prefetch=1,
            grid=(4,),
            in_specs=[pl.BlockSpec(*b) for b in blocks],
            out_specs=pl.BlockSpec(out_block, lambda p, order_ref: (p,) + (0,) * (len(out_block) - 1)),
        ),
        out_shape=out_shape,
        compiler_params=pltpu.CompilerParams(vmem_limit_bytes=16 * 2**20),
        cost_estimate=pl.CostEstimate(
            flops=0, bytes_accessed=4 * sum(a.size for a in operands), transcendentals=0
        ),
    )(order, *operands)


def ordered_gate_up(order, gate, up):
    rows = gate.shape[0] // 64

    def body(order_ref, gate_ref, up_ref, out_ref):
        for r in range(16):
            out_ref[0, r, :, :128] = gate_ref[0, order_ref[r]]
            out_ref[0, r, :, 128:] = up_ref[0, order_ref[r]]

    taken = ((1, 16, rows, 128), lambda p, order_ref: (p, 0, 0, 0))
    shape = jax.ShapeDtypeStruct((4, 16, rows, 256), gate.dtype)
    operands = [w.reshape(4, 16, rows, 128) for w in (gate, up)]
    out = ordered(order, operands, body, [taken, taken], (1, 16, rows, 256), shape)
    return out.reshape(4, 16 * rows, 256)


def ordered_down(order, down):
    feats, hidden = down.shape[0], down.shape[1] // 4

    def body(order_ref, down_ref, out_ref):
        for r in range(16):
            block = pl.ds(pl.multiple_of(order_ref[r] * 128, 128), 128)
            out_ref[0, :, r * 128 : (r + 1) * 128] = down_ref[:, block]

    taken = ((feats, hidden), lambda p, order_ref: (0, p))
    shape = jax.ShapeDtypeStruct((4, feats, hidden), down.dtype)
    return ordered(order, [down], body, [taken], (1, feats, hidden), shape)


def times_parts(w, axis, parts):
    total, at = 0.0, 0
    for part in parts:
        rows = lax.slice_in_dim(w, at, at + part.shape[0], axis=axis)
        total = total + contract(rows, part, axis, 0)
        at += part.shape[0]
    return total


def route(expert_ids):
    ids = expert_ids.T
    expert = lax.broadcasted_iota(jnp.int32, (8, ids.shape[1]), 0)
    first = ids[0][None, :] == expert
    second = ids[1][None, :] == expert
    ones = first.astype(BF) + second.astype(BF)
    n = ids.shape[1]
    before = lax.broadcasted_iota(jnp.int32, (n, n), 0) < lax.broadcasted_iota(jnp.int32, (n, n), 1)
    earlier = contract(ones, before.astype(BF), 1, 0)
    targets = []
    for k, (mine, count) in enumerate(((first, earlier), (second, earlier + first.astype(F32)))):
        slot = jnp.sum(jnp.where(mine, count, 0.0), axis=0).astype(jnp.int32)
        targets.append(jnp.where(slot < CAP, ids[k] * CAP + slot, -1))
    return targets


def local(tokens, expert_ids, routing_weights, gate_weight, up_weight, down_weight):
    zh = lax.axis_index("zh")
    feats, lanes = tokens.shape[1], 2 * CAP

    targets = route(expert_ids)
    slot = lax.broadcasted_iota(jnp.int32, (4 * CAP, tokens.shape[0]), 0)
    hits = []
    for half in range(2):
        base = jnp.where(half == 0, zh, 1 - zh) * (4 * CAP)
        hits.append([(t[None, :] - base) == slot for t in targets])
    packed = [contract(tokens, (a | b).astype(BF), 0, 1).astype(BF) for a, b in hits]
    _, gate_weight, up_weight = held(packed[1][:8], gate_weight, up_weight)
    packed[1] = lax.ppermute(packed[1], "zh", flip(2, 1))
    gate_up = ordered_gate_up(block_order(8), gate_weight[0], up_weight[0])

    v = jnp.concatenate([p.reshape(feats, 4, CAP) for p in packed], axis=2).transpose(1, 0, 2)
    v = lax.all_to_all(v, "y", 0, 0).transpose(1, 0, 2).reshape(feats, -1)
    _, gate_up, down_weight = held(v[:8, :128], gate_up, down_weight)
    gate_up = lax.all_to_all(gate_up, "x", 0, 0)
    down = ordered_down(block_order(3), down_weight[0].T)
    parts = gather_z(v, 8)
    terms = times_parts(gate_up, 1, parts).astype(BF)
    both = jnp.sum(lax.all_to_all(terms, "x", 0, 0).astype(F32), axis=0)
    gate, up = both[:128], both[128:]
    hidden = (jax.nn.silu(gate) * up).astype(BF)

    hidden, down = held(hidden, down)
    down = lax.all_to_all(down, "x", 0, 0)
    parts = gather_z(hidden, 3)
    terms = times_parts(down, 2, parts).astype(BF)
    terms = terms.reshape(4, feats, 4, lanes).transpose(2, 0, 1, 3).reshape(16, feats, lanes)
    terms = lax.all_to_all(terms, ("y", "x"), 0, 0).reshape(4, 4, feats, lanes)
    back = jnp.sum(terms.astype(F32), axis=1).astype(BF).transpose(1, 0, 2)
    backs = [back[:, :, :CAP].reshape(feats, -1), back[:, :, CAP:].reshape(feats, -1)]
    backs[1] = lax.ppermute(backs[1], "zh", flip(2, 1))

    mixed = 0.0
    for k in range(2):
        picked = sum(contract(backs[h], hits[h][k].astype(BF), 1, 0) for h in range(2))
        mixed = mixed + picked * routing_weights[:, k][None, :]
    return mixed.astype(BF).T


def solution(mesh):
    fine = Mesh(mesh.devices.reshape(2, 4, 4, 8, 2), AXES)
    rows, cols = ("zh", "y"), ("x", "z", "c")
    placed = (
        P(rows, cols),
        P(rows, None),
        P(rows, None),
        P(rows, None, cols),
        P(rows, None, cols),
        P(rows, None, cols),
    )
    return jax.shard_map(local, mesh=fine, in_specs=placed, out_specs=P(rows, cols), check_vma=False)
```

```python
import jax
import jax.numpy as jnp
from jax import lax
from jax.experimental import pallas as pl
from jax.experimental.pallas import tpu as pltpu
from jax.sharding import Mesh, PartitionSpec as P

BF = jnp.bfloat16
F32 = jnp.float32
CAP = 64
AXES = ("zh", "y", "x", "z", "c")
ORDER = (0, 4, 2, 1, 5, 3, 6, 7)


def shift(n, d):
    return [(i, (i + d) % n) for i in range(n)]


def flip(n, d):
    return [(i, i ^ d) for i in range(n)]


def contract(a, b, da, db):
    return lax.dot_general(a, b, (((da,), (db,)), ((), ())), preferred_element_type=F32)


def held(*arrays):
    return lax.optimization_barrier(arrays)


def gather_z(v, first):
    over = lambda a, step: lax.ppermute(a, "z", flip(8, step))
    core = lambda a: lax.ppermute(a, "c", flip(2, 1))
    b4, b2, b1 = over(v, 4), over(v, 2), over(v, 1)
    early = jnp.concatenate([v, b4, b2])
    b6, b53 = over(b4, 2), over(early[v.shape[0] :], 1)
    b153 = jnp.concatenate([b1, b53])
    late = [b153, b6, over(b6, 1)]
    if first == len(ORDER):
        rows = [jnp.concatenate([early] + late)]
        return rows[0], core(rows[0])
    late, early_other = held(jnp.concatenate(late), core(early))
    return early, early_other, late, core(late)


def block_order(first):
    z, c = lax.axis_index("z"), lax.axis_index("c")
    blocks = [(i, j) for some in (ORDER[:first], ORDER[first:]) for j in (0, 1) for i in some]
    return jnp.stack([(z ^ i) * 2 + (c ^ j) for i, j in blocks]).astype(jnp.int32)


def ordered(order, operands, body, blocks, out_block, out_shape):
    return pl.pallas_call(
        body,
        grid_spec=pltpu.PrefetchScalarGridSpec(
            num_scalar_prefetch=1,
            grid=(4,),
            in_specs=[pl.BlockSpec(*b) for b in blocks],
            out_specs=pl.BlockSpec(out_block, lambda p, order_ref: (p,) + (0,) * (len(out_block) - 1)),
        ),
        out_shape=out_shape,
        compiler_params=pltpu.CompilerParams(vmem_limit_bytes=16 * 2**20),
        cost_estimate=pl.CostEstimate(
            flops=0, bytes_accessed=4 * sum(a.size for a in operands), transcendentals=0
        ),
    )(order, *operands)


def ordered_gate_up(order, gate, up):
    rows = gate.shape[0] // 64

    def body(order_ref, gate_ref, up_ref, out_ref):
        for r in range(16):
            out_ref[0, r, :, :128] = gate_ref[0, order_ref[r]]
            out_ref[0, r, :, 128:] = up_ref[0, order_ref[r]]

    taken = ((1, 16, rows, 128), lambda p, order_ref: (p, 0, 0, 0))
    shape = jax.ShapeDtypeStruct((4, 16, rows, 256), gate.dtype)
    operands = [w.reshape(4, 16, rows, 128) for w in (gate, up)]
    out = ordered(order, operands, body, [taken, taken], (1, 16, rows, 256), shape)
    return out.reshape(4, 16 * rows, 256)


def ordered_down(order, down):
    feats, hidden = down.shape[0], down.shape[1] // 4

    def body(order_ref, down_ref, out_ref):
        for r in range(16):
            block = pl.ds(pl.multiple_of(order_ref[r] * 128, 128), 128)
            out_ref[0, :, r * 128 : (r + 1) * 128] = down_ref[:, block]

    taken = ((feats, hidden), lambda p, order_ref: (0, p))
    shape = jax.ShapeDtypeStruct((4, feats, hidden), down.dtype)
    return ordered(order, [down], body, [taken], (1, feats, hidden), shape)


def times_parts(w, axis, parts):
    total, at = 0.0, 0
    for part in parts:
        rows = lax.slice_in_dim(w, at, at + part.shape[0], axis=axis)
        total = total + contract(rows, part, axis, 0)
        at += part.shape[0]
    return total


def route(expert_ids):
    ids = expert_ids.T
    expert = lax.broadcasted_iota(jnp.int32, (8, ids.shape[1]), 0)
    first = ids[0][None, :] == expert
    second = ids[1][None, :] == expert
    ones = first.astype(BF) + second.astype(BF)
    n = ids.shape[1]
    before = lax.broadcasted_iota(jnp.int32, (n, n), 0) < lax.broadcasted_iota(jnp.int32, (n, n), 1)
    earlier = contract(ones, before.astype(BF), 1, 0)
    targets = []
    for k, (mine, count) in enumerate(((first, earlier), (second, earlier + first.astype(F32)))):
        slot = jnp.sum(jnp.where(mine, count, 0.0), axis=0).astype(jnp.int32)
        targets.append(jnp.where(slot < CAP, ids[k] * CAP + slot, -1))
    return targets


def local(tokens, expert_ids, routing_weights, gate_weight, up_weight, down_weight):
    zh = lax.axis_index("zh")
    feats, lanes = tokens.shape[1], 2 * CAP

    targets = route(expert_ids)
    slot = lax.broadcasted_iota(jnp.int32, (4 * CAP, tokens.shape[0]), 0)
    hits = []
    for half in range(2):
        base = jnp.where(half == 0, zh, 1 - zh) * (4 * CAP)
        hits.append([(t[None, :] - base) == slot for t in targets])
    packed = [contract(tokens, (a | b).astype(BF), 0, 1).astype(BF) for a, b in hits]
    _, gate_weight, up_weight = held(packed[1][:8], gate_weight, up_weight)
    packed[1] = lax.ppermute(packed[1], "zh", flip(2, 1))
    gate_up = ordered_gate_up(block_order(8), gate_weight[0], up_weight[0])

    v = jnp.concatenate([p.reshape(feats, 4, CAP) for p in packed], axis=2).transpose(1, 0, 2)
    v = lax.all_to_all(v, "y", 0, 0).transpose(1, 0, 2).reshape(feats, -1)
    _, gate_up, down_weight = held(v[:8, :128], gate_up, down_weight)
    gate_up = lax.all_to_all(gate_up, "x", 0, 0)
    down = ordered_down(block_order(8), down_weight[0].T)
    parts = gather_z(v, 8)
    terms = times_parts(gate_up, 1, parts).astype(BF)
    both = jnp.sum(lax.all_to_all(terms, "x", 0, 0).astype(F32), axis=0)
    gate, up = both[:128], both[128:]
    hidden = (jax.nn.silu(gate) * up).astype(BF)

    hidden, down = held(hidden, down)
    down = lax.all_to_all(down, "x", 0, 0)
    parts = gather_z(hidden, 8)
    terms = times_parts(down, 2, parts).astype(BF)
    terms = terms.reshape(4, feats, 4, lanes).transpose(2, 0, 1, 3).reshape(16, feats, lanes)
    terms = lax.all_to_all(terms, ("y", "x"), 0, 0).reshape(4, 4, feats, lanes)
    back = jnp.sum(terms.astype(F32), axis=1).astype(BF).transpose(1, 0, 2)
    backs = [back[:, :, :CAP].reshape(feats, -1), back[:, :, CAP:].reshape(feats, -1)]
    backs[1] = lax.ppermute(backs[1], "zh", flip(2, 1))

    mixed = 0.0
    for k in range(2):
        picked = sum(contract(backs[h], hits[h][k].astype(BF), 1, 0) for h in range(2))
        mixed = mixed + picked * routing_weights[:, k][None, :]
    return mixed.astype(BF).T


def solution(mesh):
    fine = Mesh(mesh.devices.reshape(2, 4, 4, 8, 2), AXES)
    rows, cols = ("zh", "y"), ("x", "z", "c")
    placed = (
        P(rows, cols),
        P(rows, None),
        P(rows, None),
        P(rows, None, cols),
        P(rows, None, cols),
        P(rows, None, cols),
    )
    return jax.shard_map(local, mesh=fine, in_specs=placed, out_specs=P(rows, cols), check_vma=False)
```
